512 devices in a mesh: dp: 16 (over z), seq: 32 (over x, y, core).
Axes of the slice: x: 4, y: 4, z: 16, core: 2. Of those that a mesh axis runs over, the one named last changes fastest.
Arguments:
- queries: bfloat16 [16, 4096, 2048], P('dp', 'seq'), may hold values from -90 to 90
- keys: bfloat16 [16, 4096, 2048], P('dp', 'seq'), may hold values from -6 to 6
- values: bfloat16 [16, 4096, 2048], P('dp', 'seq'), may hold values from -6 to 6
- d_out: bfloat16 [16, 4096, 2048], P('dp', 'seq'), may hold values from -6 to 6
- cluster_ids: int32 [16, 4096, 16], P('dp', 'seq'), may hold values from 0 to 63, as said below
- gain: float32 [2048], replicated, may hold values from 0.1 to 1.9
Outputs:
- query_grad: bfloat16 [16, 4096, 2048], P('dp', 'seq')
- key_grad: bfloat16 [16, 4096, 2048], P('dp', 'seq')
- value_grad: bfloat16 [16, 4096, 2048], P('dp', 'seq')
- gain_grad: float32 [2048], replicated
The draws below stay inside these ranges and needn't reach their ends.
Inputs may be any that keep to these rules, and one draw needn't show every extreme that they name: `cluster_ids`: cluster c belongs to owner c // 2. For every sequence and head, the 128 positions held by one seq index name clusters of every owner, exactly 4 positions for each.
All inputs are finite; a program needn't handle non-finite values.
Results may differ from the reference program's by a relative error of at most 0.0067.
Values may be sent and summed in bfloat16 or wider, within the bound.
A program may use at most 64 MiB of HBM per device.

```python
import jax
import jax.numpy as jnp
from jax import lax

H = 16
HD = 128
TOK_DEV = 128
CPO = 2
MOST = 4
SEQLEN = 4096
BATCH = 16
N_SEQ = 32


def shared_normal(key):
    return jnp.clip(jax.random.normal(key, (BATCH, SEQLEN, H * HD), jnp.float32), -6.0, 6.0)


def draw_keys(key, part):
    common = shared_normal(key)
    return common.astype(jnp.bfloat16)


def draw_queries(key, part):
    key = jax.random.fold_in(key, 12)
    own = jnp.clip(jax.random.normal(key, (BATCH, SEQLEN, H * HD), jnp.float32), -6.0, 6.0)
    return own.astype(jnp.bfloat16)


def draw_cluster_ids(key, part):
    key = jax.random.fold_in(key, 13)
    table_key, rows_key = jax.random.split(key)
    rotate = jax.random.randint(table_key, (H, N_SEQ), 0, CPO)
    blocks = BATCH * N_SEQ
    block_keys = jax.random.split(rows_key, blocks * H)
    head_of = jnp.tile(jnp.arange(H), blocks)

    def one_block(block_key, head):
        first, third = jax.random.split(block_key, 2)
        ranks = jax.random.permutation(first, TOK_DEV)
        owner = ranks // MOST
        heavy = (jax.random.randint(third, (TOK_DEV,), 0, 5) == 0).astype(jnp.int32)
        local = (heavy + rotate[head, owner]) % CPO
        return owner * CPO + local
    grid = jax.vmap(one_block)(block_keys, head_of)
    grid = grid.reshape(BATCH, N_SEQ, H, TOK_DEV).transpose(0, 1, 3, 2).reshape(BATCH, SEQLEN, H)
    return grid.astype(jnp.int32)


def block_levels(rng, shape, shards, low, largest):
    level = 1.0
    for axis_at, parts in shards:
        heights = jax.random.uniform(jax.random.fold_in(jax.random.fold_in(rng, 6), axis_at), (parts,), jnp.float32, low / len(shards), largest / len(shards))
        level = level * jnp.repeat(jnp.exp(heights), shape[axis_at] // parts).reshape((-1,) + (1,) * (len(shape) - 1 - axis_at))
    return level


def bell_draw(key, extent, spread, bound, cuts=(), kind=jnp.bfloat16):
    loudness = block_levels(key, extent, cuts, -0.22, 0.18) if cuts else 1.0
    entries = jax.random.normal(key, extent, jnp.float32) * spread * loudness
    return jnp.minimum(jnp.maximum(entries, -bound), bound).astype(kind)


def setup_inputs(seed: int = 0) -> dict:
    arg_keys = jax.random.split(jax.random.key(seed), 7)
    queries = draw_queries(jax.random.fold_in(arg_keys[6], 71), 0)
    keys = draw_keys(jax.random.fold_in(arg_keys[6], 71), 0)
    values = bell_draw(arg_keys[2], (BATCH, SEQLEN, H * HD), 1.0, 6.0, ((0, 16), (1, 32)))
    d_out = bell_draw(arg_keys[3], (BATCH, SEQLEN, H * HD), 1.0, 6.0, ((0, 16), (1, 32)))
    cluster_ids = draw_cluster_ids(jax.random.fold_in(arg_keys[6], 71), 0)
    gain = jnp.clip(1.0 + 0.18 * jax.random.normal(arg_keys[5], (H * HD,), jnp.float32), 0.1, 1.9)
    return {"queries": queries, "keys": keys, "values": values, "d_out": d_out, "cluster_ids": cluster_ids, "gain": gain}


def head_grads(payload):
    query, keys_raw, scaled, value, upstream, labels, gain_row = payload
    factor = HD ** -0.5
    scores = jnp.dot(query, scaled.T, preferred_element_type=jnp.float32) * factor
    positions = jnp.arange(query.shape[0])
    allowed = (labels[:, None] == labels[None, :]) & (positions[None, :] <= positions[:, None])
    scores = jnp.where(allowed, scores, -jnp.inf)
    maximum = jnp.max(scores, axis=1, keepdims=True)
    expo = jnp.where(allowed, jnp.exp(scores - maximum), 0.0)
    weights = expo / jnp.sum(expo, axis=1, keepdims=True)
    rounded = weights.astype(jnp.bfloat16)
    output = jnp.dot(rounded, value, preferred_element_type=jnp.float32)
    deltas = jnp.sum(upstream.astype(jnp.float32) * output, axis=1)
    value_grad = jnp.dot(rounded.T, upstream, preferred_element_type=jnp.float32).astype(jnp.bfloat16)
    inner = jnp.dot(upstream, value.T, preferred_element_type=jnp.float32)
    score_grad = (weights * (inner - deltas[:, None])).astype(jnp.bfloat16)
    query_grad = (jnp.dot(score_grad, scaled, preferred_element_type=jnp.float32) * factor).astype(jnp.bfloat16)
    scaled_grad = (jnp.dot(score_grad.T, query, preferred_element_type=jnp.float32) * factor).astype(jnp.bfloat16)
    key_grad = (gain_row * scaled_grad.astype(jnp.float32)).astype(jnp.bfloat16)
    gain_part = jnp.sum(keys_raw.astype(jnp.float32) * scaled_grad.astype(jnp.float32), axis=0)
    return query_grad, key_grad, value_grad, gain_part


def reference(queries, keys, values, d_out, cluster_ids, gain):
    batch_count = queries.shape[0]
    length = queries.shape[1]

    def split_heads(array):
        return array.reshape(batch_count, length, H, HD).transpose(0, 2, 1, 3).reshape(batch_count * H, length, HD)

    def join_heads(array):
        return array.reshape(batch_count, H, length, HD).transpose(0, 2, 1, 3).reshape(batch_count, length, H * HD)

    scaled_keys = (keys.astype(jnp.float32) * gain).astype(jnp.bfloat16)
    labels = cluster_ids.transpose(0, 2, 1).reshape(batch_count * H, length)
    gain_rows = jnp.tile(gain.reshape(H, HD), (batch_count, 1))
    query_grad, key_grad, value_grad, gain_parts = lax.map(
        head_grads,
        (split_heads(queries), split_heads(keys), split_heads(scaled_keys), split_heads(values),
         split_heads(d_out), labels, gain_rows))
    gain_grad = jnp.sum(gain_parts.reshape(batch_count, H * HD), axis=0)
    return join_heads(query_grad), join_heads(key_grad), join_heads(value_grad), gain_grad
```

```python
import jax
import jax.numpy as jnp
from jax import lax
from jax.experimental import pallas as pl
from jax.experimental.pallas import tpu as pltpu
from jax.sharding import PartitionSpec as P

H = 16
HD = 128
CPO = 2
MOST = 4
TOK = 128
N_SEQ = 32
N_DP = 16
GH = 4
NG = H // GH
ROWS = N_SEQ * GH * MOST
MSG = GH * MOST
WIDE = 4 * HD
BACK = 3 * HD
MESH = pl.DeviceIdType.MESH
F32 = jnp.float32
BF16 = jnp.bfloat16
NEG = -1e30


def iota(shape, dim):
    return lax.broadcasted_iota(jnp.int32, shape, dim)


def dot(a, b):
    return lax.dot_general(a, b, (((1,), (0,)), ((), ())), preferred_element_type=F32)


def dot_nt(a, b):
    return lax.dot_general(a, b, (((1,), (1,)), ((), ())), preferred_element_type=F32)


def dot_tn(a, b):
    return lax.dot_general(a, b, (((0,), (0,)), ((), ())), preferred_element_type=F32)


def kernel(
    q_hbm, k_hbm, v_hbm, d_hbm, cid_hbm, gain_hbm,
    dq_hbm, dk_hbm, dv_hbm, gg_hbm,
    xin, cid_v, gain_v, place, back_place, outbox, inbox, ret_out, ret_in,
    lab_out, lab_in, rmat, dmat, out_v,
    gp, g_recv, g_mid, z_recv, g_row, g_fin,
    in_sem, small_sem, self_sem, ret_self_sem, lab_self_sem, g_self_sem,
    f_send, f_recv, b_send, b_recv, l_send, l_recv,
    g1_send, g1_recv, g2_send, g2_recv, g3_send, g3_recv, out_sem,
):
    me = lax.axis_index("seq")
    dp = lax.axis_index("dp")
    core = me % 2
    my = (me // 2) % 4
    mx = me // 8
    chip = me // 2

    def peer(k):
        dx, dy, dc = k // 8, (k // 2) % 4, k % 2
        return ((mx + dx) % 4) * 8 + ((my + dy) % 4) * 2 + (core + dc) % 2

    def loop(lo, hi, body):
        def step(i, carry):
            body(i)
            return carry

        lax.fori_loop(lo, hi, step, 0)

    barrier = pltpu.get_barrier_semaphore()
    loop(1, N_SEQ, lambda k: pl.semaphore_signal(
        barrier, inc=1, device_id=(dp, peer(k)), device_id_type=MESH))
    loop(1, N_DP, lambda k: pl.semaphore_signal(
        barrier, inc=1, device_id=((dp + k) % N_DP, me), device_id_type=MESH))

    cid_copy = pltpu.make_async_copy(cid_hbm.at[0], cid_v, small_sem.at[0])
    cid_copy.start()
    gain_copy = pltpu.make_async_copy(gain_hbm, gain_v, small_sem.at[1])
    gain_copy.start()

    def load(g):
        cols = pl.ds(pl.multiple_of(g * GH * HD, GH * HD), GH * HD)
        for t, ref in enumerate((q_hbm, k_hbm, v_hbm, d_hbm)):
            pltpu.make_async_copy(ref.at[0, :, cols], xin.at[g, t], in_sem.at[g]).start()

    loop(0, NG, load)
    cid_copy.wait()
    cid = cid_v[...].astype(F32).astype(BF16)

    def select(g):
        r = iota((ROWS, H), 0)
        return jnp.where(iota((ROWS, H), 1) == GH * g + (r // MOST) % GH, 1.0, 0.0).astype(BF16)

    def head_of(shape, dim):
        return (iota(shape, dim) // MOST) % GH

    def make_place(g):
        shape = (ROWS, TOK)
        r = iota(shape, 0)
        label = dot_nt(select(g), cid) - (CPO * (r // MSG)).astype(F32)
        member = (label == 0.0) | (label == 1.0)
        before = jnp.where(iota((TOK, TOK), 0) < iota((TOK, TOK), 1), 1.0, 0.0).astype(BF16)
        rank = dot(jnp.where(member, 1.0, 0.0).astype(BF16), before)
        chosen = member & (rank == (r % MOST).astype(F32))
        place[g] = jnp.where(chosen, 1.0, 0.0).astype(BF16)
        row_label = dot(
            jnp.where(chosen, label, 0.0).astype(BF16), jnp.ones((TOK, TOK), BF16)
        )
        spread = jnp.where(iota(shape, 1) == MSG * g + r % MSG, row_label, 0.0).astype(BF16)
        owners = jnp.where(
            iota((N_SEQ, ROWS), 1) // MSG == iota((N_SEQ, ROWS), 0), 1.0, 0.0
        ).astype(BF16)
        return dot(owners, spread)

    def make_back(g):
        shape = (TOK, ROWS)
        r = iota(shape, 1)
        label = dot_nt(cid, select(g)) - (CPO * (r // MSG)).astype(F32)
        member = (label == 0.0) | (label == 1.0)
        before = jnp.where(iota((TOK, TOK), 1) < iota((TOK, TOK), 0), 1.0, 0.0).astype(BF16)
        rank = dot(before, jnp.where(member, 1.0, 0.0).astype(BF16))
        chosen = member & (rank == (r % MOST).astype(F32))
        back_place[g] = jnp.where(chosen, 1.0, 0.0).astype(BF16)

    def pack(g):
        pltpu.make_async_copy(xin.at[g], xin.at[g], in_sem.at[g]).wait()
        head = head_of((ROWS, TOK), 0)
        chosen = place[g]
        zero = jnp.zeros_like(chosen)
        left = jnp.concatenate([jnp.where(head == h, chosen, zero) for h in range(GH)], axis=1)
        for t in range(4):
            stack = jnp.concatenate(
                [xin[g, t, :, h * HD : (h + 1) * HD] for h in range(GH)], axis=0
            )
            outbox[g, :, :, t * HD : (t + 1) * HD] = (
                dot(left, stack).astype(BF16).reshape(N_SEQ, MSG, HD)
            )

    def forward(g, k):
        to = peer(k)
        return pltpu.make_async_remote_copy(
            src_ref=outbox.at[g, to], dst_ref=inbox.at[g, me],
            send_sem=f_send.at[g], recv_sem=f_recv.at[g],
            device_id=(dp, to), device_id_type=MESH)

    def send_forward(g):
        loop(1, N_SEQ, lambda k: forward(g, k).start())
        pltpu.make_async_copy(outbox.at[g, me], inbox.at[g, me], self_sem.at[g]).start()

    def forward_all(g):
        return pltpu.make_async_remote_copy(
            src_ref=outbox.at[g, pl.ds(0, N_SEQ - 1)], dst_ref=inbox.at[g, pl.ds(0, N_SEQ - 1)],
            send_sem=f_send.at[g], recv_sem=f_recv.at[g],
            device_id=(dp, peer(1)), device_id_type=MESH)

    def back_all(g):
        return pltpu.make_async_remote_copy(
            src_ref=ret_out.at[g, pl.ds(0, N_SEQ - 1)], dst_ref=ret_in.at[g, pl.ds(0, N_SEQ - 1)],
            send_sem=b_send.at[g], recv_sem=b_recv.at[g],
            device_id=(dp, peer(1)), device_id_type=MESH)

    def label_all():
        return pltpu.make_async_remote_copy(
            src_ref=lab_out.at[pl.ds(0, N_SEQ - 1)], dst_ref=lab_in.at[pl.ds(0, N_SEQ - 1)],
            send_sem=l_send, recv_sem=l_recv,
            device_id=(dp, peer(1)), device_id_type=MESH)

    labels = make_place(0)
    pack(0)
    pl.semaphore_wait(barrier, N_SEQ - 1 + N_DP - 1)
    send_forward(0)

    labels = lax.fori_loop(1, NG, lambda g, acc: acc + make_place(g), labels)
    lab_out[...] = labels

    def send_label(k):
        to = peer(k)
        pltpu.make_async_remote_copy(
            src_ref=lab_out.at[pl.ds(to, 1)], dst_ref=lab_in.at[pl.ds(me, 1)],
            send_sem=l_send, recv_sem=l_recv,
            device_id=(dp, to), device_id_type=MESH).start()

    loop(1, N_SEQ, send_label)
    lab_self = pltpu.make_async_copy(
        lab_out.at[pl.ds(me, 1)], lab_in.at[pl.ds(me, 1)], lab_self_sem)
    lab_self.start()

    def pack_send(g):
        pack(g)
        send_forward(g)

    loop(1, NG, pack_send)
    loop(0, NG, make_back)
    gain_copy.wait()
    label_all().wait_recv()
    lab_self.wait()

    factor = HD ** (-0.5)

    def attend(g):
        forward_all(g).wait_recv()
        pltpu.make_async_copy(outbox.at[g, me], inbox.at[g, me], self_sem.at[g]).wait()
        shape = (ROWS, HD)
        r = iota(shape, 0)
        head = head_of(shape, 0)
        gain_rows = jnp.zeros(shape, F32)
        for h in range(GH):
            gain_rows = jnp.where(head == h, gain_v[pl.ds(GH * g + h, 1), :], gain_rows)
        from_src = jnp.where(
            iota((ROWS, N_SEQ), 0) // MSG == iota((ROWS, N_SEQ), 1), 1.0, 0.0
        ).astype(BF16)
        arrived = dot(from_src, lab_in[...].astype(BF16))
        arrived = jnp.where(iota(shape, 1) == MSG * g + r % MSG, arrived, 0.0).astype(BF16)
        code_col = dot(arrived, jnp.ones((HD, HD), BF16)) + (2 * head).astype(F32)
        code_row = dot_nt(jnp.ones((8, HD), BF16), arrived)[0:1, :] + (
            2 * head_of((1, ROWS), 1)
        ).astype(F32)

        def part(t, lo, hi):
            n = hi - lo
            return inbox[g, lo // MSG : hi // MSG, :, t * HD : (t + 1) * HD].reshape(n, HD)

        query = part(0, 0, ROWS)
        raw = part(1, 0, ROWS).astype(F32)
        value = part(2, 0, ROWS)
        upstream = part(3, 0, ROWS)
        scaled = (raw * gain_rows).astype(BF16)
        for i in range(GH):
            lo, hi = i * 128, (i + 1) * 128
            scores = dot_nt(scaled[:hi], query[lo:hi]) * factor
            allowed = (code_col[:hi] == code_row[:, lo:hi]) & (
                iota((hi, 128), 0) <= iota((hi, 128), 1) + lo
            )
            scores = jnp.where(allowed, scores, NEG)
            expo = jnp.exp(scores - jnp.max(scores, axis=0, keepdims=True))
            weights = expo * (1.0 / jnp.sum(expo, axis=0, keepdims=True))
            rounded = weights.astype(BF16)
            rmat[:hi, lo:hi] = rounded
            inner = dot_nt(value[:hi], upstream[lo:hi])
            delta = jnp.sum(rounded.astype(F32) * inner, axis=0, keepdims=True)
            grad = (weights * (inner - delta)).astype(BF16)
            dmat[:hi, lo:hi] = grad
            query_grad = (dot_tn(grad, scaled[:hi]) * factor).astype(BF16)
            ret_out[g, lo // MSG : hi // MSG, :, 0:HD] = query_grad.reshape(
                128 // MSG, MSG, HD)
        total = jnp.zeros((MSG, HD), F32)
        for j in range(GH):
            lo, hi = j * 128, (j + 1) * 128
            value_grad = dot(rmat[lo:hi, lo:], upstream[lo:]).astype(BF16)
            ret_out[g, lo // MSG : hi // MSG, :, 2 * HD : 3 * HD] = value_grad.reshape(
                128 // MSG, MSG, HD)
            scaled_grad = (dot(dmat[lo:hi, lo:], query[lo:]) * factor).astype(BF16).astype(F32)
            key_grad = (gain_rows[lo:hi] * scaled_grad).astype(BF16)
            ret_out[g, lo // MSG : hi // MSG, :, HD : 2 * HD] = key_grad.reshape(
                128 // MSG, MSG, HD)
            total = total + jnp.sum((raw[lo:hi] * scaled_grad).reshape(128 // MSG, MSG, HD), axis=0)

        def send_back(k):
            to = peer(k)
            pltpu.make_async_remote_copy(
                src_ref=ret_out.at[g, to], dst_ref=ret_in.at[g, me],
                send_sem=b_send.at[g], recv_sem=b_recv.at[g],
                device_id=(dp, to), device_id_type=MESH).start()

        loop(1, N_SEQ, send_back)
        pltpu.make_async_copy(ret_out.at[g, me], ret_in.at[g, me], ret_self_sem.at[g]).start()
        rows16 = iota((MSG, HD), 0) // MOST
        for h in range(GH):
            gp[pl.ds(GH * g + h, 1), :] = jnp.sum(
                jnp.where(rows16 == h, total, 0.0), axis=0, keepdims=True)

    loop(0, NG, attend)

    def gain_one(c):
        @pl.when(2 * c != me)
        def _():
            pltpu.make_async_remote_copy(
                src_ref=gp.at[pl.ds(c, 1)], dst_ref=g_recv.at[pl.ds(me, 1)],
                send_sem=g1_send, recv_sem=g1_recv,
                device_id=(dp, 2 * c), device_id_type=MESH).start()

    loop(0, H, gain_one)

    def unpack(g):
        back_all(g).wait_recv()
        pltpu.make_async_copy(ret_out.at[g, me], ret_in.at[g, me], ret_self_sem.at[g]).wait()
        head = head_of((TOK, ROWS), 1)
        chosen = back_place[g]
        zero = jnp.zeros_like(chosen)
        left = jnp.concatenate([jnp.where(head == h, chosen, zero) for h in range(GH)], axis=0)
        home = dot(left, ret_in[g].reshape(ROWS, BACK)).astype(BF16)
        cols = pl.ds(pl.multiple_of(g * GH * HD, GH * HD), GH * HD)
        for t, ref in enumerate((dq_hbm, dk_hbm, dv_hbm)):
            for h in range(GH):
                out_v[g, t, :, h * HD : (h + 1) * HD] = home[
                    h * TOK : (h + 1) * TOK, t * HD : (t + 1) * HD]
            pltpu.make_async_copy(out_v.at[g, t], ref.at[0, :, cols], out_sem.at[g]).start()

    def rows_copy(src, dst, n, send, recv):
        return pltpu.make_async_remote_copy(
            src_ref=src.at[pl.ds(0, n)], dst_ref=dst.at[pl.ds(0, n)], send_sem=send, recv_sem=recv,
            device_id=(dp, peer(1)), device_id_type=MESH)

    unpack(0)

    @pl.when(core == 0)
    def _():
        own = pltpu.make_async_copy(
            gp.at[pl.ds(chip, 1)], g_recv.at[pl.ds(me, 1)], g_self_sem.at[0])
        own.start()
        rows_copy(g_recv, g_recv, N_SEQ - 1, g1_send, g1_recv).wait_recv()
        own.wait()
        g_mid[...] = jnp.broadcast_to(jnp.sum(g_recv[...], axis=0, keepdims=True), g_mid.shape)

        def gain_two(k):
            pltpu.make_async_remote_copy(
                src_ref=g_mid.at[pl.ds(0, 1)], dst_ref=z_recv.at[pl.ds(dp, 1)],
                send_sem=g2_send, recv_sem=g2_recv,
                device_id=((dp + k) % N_DP, me), device_id_type=MESH).start()

        loop(1, N_DP, gain_two)
        pltpu.make_async_copy(
            g_mid.at[pl.ds(0, 1)], z_recv.at[pl.ds(dp, 1)], g_self_sem.at[1]).start()

    unpack(1)

    @pl.when(core == 0)
    def _():
        rows_copy(z_recv, z_recv, N_DP - 1, g2_send, g2_recv).wait()
        pltpu.make_async_copy(
            g_mid.at[pl.ds(0, 1)], z_recv.at[pl.ds(dp, 1)], g_self_sem.at[1]).wait()
        g_row[...] = jnp.broadcast_to(jnp.sum(z_recv[...], axis=0, keepdims=True), g_row.shape)

        def gain_three(k):
            pltpu.make_async_remote_copy(
                src_ref=g_row.at[pl.ds(0, 1)], dst_ref=g_fin.at[pl.ds(chip, 1)],
                send_sem=g3_send, recv_sem=g3_recv,
                device_id=(dp, peer(k)), device_id_type=MESH).start()

        loop(1, N_SEQ, gain_three)
        own = pltpu.make_async_copy(
            g_row.at[pl.ds(0, 1)], g_fin.at[pl.ds(chip, 1)], g_self_sem.at[0])
        own.start()
        own.wait()

    unpack(2)
    unpack(3)

    @pl.when(core == 0)
    def _():
        rows_copy(gp, gp, H - 1, g1_send, g1_recv).wait_send()
        rows_copy(g_fin, g_fin, H - 1, g3_send, g3_recv).wait_recv()
        rows_copy(g_recv, g_recv, N_SEQ - 1, g3_send, g3_recv).wait_send()

    @pl.when(core == 1)
    def _():
        rows_copy(gp, gp, H, g1_send, g1_recv).wait_send()
        rows_copy(g_fin, g_fin, H, g3_send, g3_recv).wait_recv()

    gain_out = pltpu.make_async_copy(g_fin, gg_hbm, small_sem.at[0])
    gain_out.start()

    def finish(g):
        forward_all(g).wait_send()
        back_all(g).wait_send()
        pltpu.make_async_copy(out_v.at[g], out_v.at[g], out_sem.at[g]).wait()

    loop(0, NG, finish)
    label_all().wait_send()
    gain_out.wait()


def on_device(queries, keys, values, d_out, cluster_ids, gain):
    anywhere = pl.BlockSpec(memory_space=pl.ANY)
    rows = jax.ShapeDtypeStruct(queries.shape, BF16)
    dma = pltpu.SemaphoreType.DMA
    query_grad, key_grad, value_grad, gain_grad = pl.pallas_call(
        kernel,
        out_shape=(rows, rows, rows, jax.ShapeDtypeStruct((H, HD), F32)),
        in_specs=[anywhere] * 6,
        out_specs=(anywhere,) * 4,
        scratch_shapes=[
            pltpu.VMEM((NG, 4, TOK, GH * HD), BF16),
            pltpu.VMEM((TOK, H), jnp.int32),
            pltpu.VMEM((H, HD), F32),
            pltpu.VMEM((NG, ROWS, TOK), BF16),
            pltpu.VMEM((NG, TOK, ROWS), BF16),
            pltpu.VMEM((NG, N_SEQ, MSG, WIDE), BF16),
            pltpu.VMEM((NG, N_SEQ, MSG, WIDE), BF16),
            pltpu.VMEM((NG, N_SEQ, MSG, BACK), BF16),
            pltpu.VMEM((NG, N_SEQ, MSG, BACK), BF16),
            pltpu.VMEM((N_SEQ, HD), F32),
            pltpu.VMEM((N_SEQ, HD), F32),
            pltpu.VMEM((ROWS, ROWS), BF16),
            pltpu.VMEM((ROWS, ROWS), BF16),
            pltpu.VMEM((NG, 3, TOK, GH * HD), BF16),
            pltpu.VMEM((H, HD), F32),
            pltpu.VMEM((N_SEQ, HD), F32),
            pltpu.VMEM((8, HD), F32),
            pltpu.VMEM((N_DP, HD), F32),
            pltpu.VMEM((8, HD), F32),
            pltpu.VMEM((H, HD), F32),
            dma((NG,)), dma((2,)), dma((NG,)), dma((NG,)), dma, dma((2,)),
            dma((NG,)), dma((NG,)), dma((NG,)), dma((NG,)), dma, dma,
            dma, dma, dma, dma, dma, dma, dma((NG,)),
        ],
        compiler_params=pltpu.CompilerParams(
            collective_id=0, has_side_effects=True, vmem_limit_bytes=48 * 2**20
        ),
    )(queries, keys, values, d_out, cluster_ids, gain.reshape(H, HD))
    return query_grad, key_grad, value_grad, gain_grad.reshape(H * HD)


def solution(mesh):
    rows = P("dp", "seq", None)
    return jax.shard_map(
        on_device, mesh=mesh, in_specs=(rows,) * 5 + (P(),),
        out_specs=(rows, rows, rows, P()), check_vma=False,
    )
```

```python
import jax
import jax.numpy as jnp
from jax import lax
from jax.experimental import pallas as pl
from jax.experimental.pallas import tpu as pltpu
from jax.sharding import PartitionSpec as P

H = 16
HD = 128
CPO = 2
MOST = 4
TOK = 128
N_SEQ = 32
N_DP = 16
GH = 4
NG = H // GH
ROWS = N_SEQ * GH * MOST
MSG = GH * MOST
WIDE = 4 * HD
BACK = 3 * HD
MESH = pl.DeviceIdType.MESH
F32 = jnp.float32
BF16 = jnp.bfloat16
NEG = -1e30


def iota(shape, dim):
    return lax.broadcasted_iota(jnp.int32, shape, dim)


def dot(a, b):
    return lax.dot_general(a, b, (((1,), (0,)), ((), ())), preferred_element_type=F32)


def dot_nt(a, b):
    return lax.dot_general(a, b, (((1,), (1,)), ((), ())), preferred_element_type=F32)


def dot_tn(a, b):
    return lax.dot_general(a, b, (((0,), (0,)), ((), ())), preferred_element_type=F32)


def kernel(
    q_hbm, k_hbm, v_hbm, d_hbm, cid_hbm, gain_v,
    dq_ref, dk_ref, dv_ref, gg_ref,
    xin, cid_v, place, back_place, outbox, inbox, ret_out, ret_in,
    lab_out, lab_in, rmat, dmat,
    gp, c_in, chip_sum, z_in, z_sum, p_in,
    in_sem, small_sem, self_sem, ret_self_sem, lab_self_sem, go_sem,
    f_send, f_recv, b_send, b_recv, l_send, l_recv,
    c_send, c_recv, z_send, z_recv, p_send, p_recv,
):
    me = lax.axis_index("seq")
    dp = lax.axis_index("dp")
    core = me % 2
    my = (me // 2) % 4
    mx = me // 8
    chip = me // 2

    def peer(k):
        dx, dy, dc = k // 8, (k // 2) % 4, k % 2
        return ((mx + dx) % 4) * 8 + ((my + dy) % 4) * 2 + (core + dc) % 2

    def loop(lo, hi, body):
        def step(i, carry):
            body(i)
            return carry

        lax.fori_loop(lo, hi, step, 0)

    barrier = pltpu.get_barrier_semaphore()
    sibling = (dp, chip * 2 + 1 - core)

    def greet_plane(c):
        @pl.when(2 * c != me)
        def _():
            pl.semaphore_signal(barrier, inc=1, device_id=(dp, 2 * c), device_id_type=MESH)

    loop(0, N_SEQ // 2, greet_plane)

    @pl.when(core == 1)
    def _():
        loop(1, N_DP, lambda k: pl.semaphore_signal(
            barrier, inc=1, device_id=((dp + k) % N_DP, me), device_id_type=MESH))

    cid_copy = pltpu.make_async_copy(cid_hbm.at[0], cid_v, small_sem)
    cid_copy.start()

    def load(g):
        cols = pl.ds(pl.multiple_of(g * GH * HD, GH * HD), GH * HD)
        for t, ref in enumerate((q_hbm, k_hbm, v_hbm, d_hbm)):
            pltpu.make_async_copy(ref.at[0, :, cols], xin.at[g, t], in_sem.at[g]).start()

    loop(0, NG, load)
    cid_copy.wait()
    cid = cid_v[...].astype(F32).astype(BF16)

    def select(g):
        r = iota((ROWS, H), 0)
        return jnp.where(iota((ROWS, H), 1) == GH * g + (r // MOST) % GH, 1.0, 0.0).astype(BF16)

    def select_back(g):
        r = iota((H, ROWS), 1)
        return jnp.where(iota((H, ROWS), 0) == GH * g + (r // MOST) % GH, 1.0, 0.0).astype(BF16)

    def head_of(shape, dim):
        return (iota(shape, dim) // MOST) % GH

    def make_place(g):
        shape = (ROWS, TOK)
        r = iota(shape, 0)
        label = dot(select(g), cid) - (CPO * (r // MSG)).astype(F32)
        member = (label == 0.0) | (label == 1.0)
        before = jnp.where(iota((TOK, TOK), 0) < iota((TOK, TOK), 1), 1.0, 0.0).astype(BF16)
        rank = dot(jnp.where(member, 1.0, 0.0).astype(BF16), before)
        chosen = member & (rank == (r % MOST).astype(F32))
        place[g] = jnp.where(chosen, 1.0, 0.0).astype(BF16)
        row_label = dot(
            jnp.where(chosen, label, 0.0).astype(BF16), jnp.ones((TOK, TOK), BF16)
        )
        spread = jnp.where(iota(shape, 1) == MSG * g + r % MSG, row_label, 0.0).astype(BF16)
        owners = jnp.where(
            iota((N_SEQ, ROWS), 1) // MSG == iota((N_SEQ, ROWS), 0), 1.0, 0.0
        ).astype(BF16)
        return dot(owners, spread)

    def make_back(g):
        shape = (TOK, ROWS)
        r = iota(shape, 1)
        label = dot_tn(cid, select_back(g)) - (CPO * (r // MSG)).astype(F32)
        member = (label == 0.0) | (label == 1.0)
        before = jnp.where(iota((TOK, TOK), 1) < iota((TOK, TOK), 0), 1.0, 0.0).astype(BF16)
        rank = dot(before, jnp.where(member, 1.0, 0.0).astype(BF16))
        chosen = member & (rank == (r % MOST).astype(F32))
        back_place[g] = jnp.where(chosen, 1.0, 0.0).astype(BF16)

    def pack(g):
        pltpu.make_async_copy(xin.at[g], xin.at[g], in_sem.at[g]).wait()
        head = head_of((ROWS, TOK), 0)
        chosen = place[g]
        zero = jnp.zeros_like(chosen)
        left = jnp.concatenate([jnp.where(head == h, chosen, zero) for h in range(GH)], axis=1)
        for t in range(4):
            stack = jnp.concatenate(
                [xin[g, t, :, h * HD : (h + 1) * HD] for h in range(GH)], axis=0
            )
            outbox[g, :, :, t * HD : (t + 1) * HD] = (
                dot(left, stack).astype(BF16).reshape(N_SEQ, MSG, HD)
            )

    def forward(g, k):
        to = peer(k)
        return pltpu.make_async_remote_copy(
            src_ref=outbox.at[g, to], dst_ref=inbox.at[g, me],
            send_sem=f_send.at[g], recv_sem=f_recv.at[g],
            device_id=(dp, to), device_id_type=MESH)

    def send_forward(g):
        loop(1, N_SEQ, lambda k: forward(g, k).start())
        pltpu.make_async_copy(outbox.at[g, me], inbox.at[g, me], self_sem.at[g]).start()

    def forward_all(g):
        return pltpu.make_async_remote_copy(
            src_ref=outbox.at[g, pl.ds(0, N_SEQ - 1)], dst_ref=inbox.at[g, pl.ds(0, N_SEQ - 1)],
            send_sem=f_send.at[g], recv_sem=f_recv.at[g],
            device_id=(dp, peer(1)), device_id_type=MESH)

    def back_all(g):
        return pltpu.make_async_remote_copy(
            src_ref=ret_out.at[g, pl.ds(0, N_SEQ - 1)], dst_ref=ret_in.at[g, pl.ds(0, N_SEQ - 1)],
            send_sem=b_send.at[g], recv_sem=b_recv.at[g],
            device_id=(dp, peer(1)), device_id_type=MESH)

    def label_all():
        return pltpu.make_async_remote_copy(
            src_ref=lab_out.at[pl.ds(0, N_SEQ - 1)], dst_ref=lab_in.at[pl.ds(0, N_SEQ - 1)],
            send_sem=l_send, recv_sem=l_recv,
            device_id=(dp, peer(1)), device_id_type=MESH)

    labels = make_place(0)
    pack(0)

    @pl.when(core == 0)
    def _():
        pl.semaphore_wait(barrier, N_SEQ - 1)
        pl.semaphore_signal(go_sem, inc=1, device_id=sibling, device_id_type=MESH)

    @pl.when(core == 1)
    def _():
        pl.semaphore_wait(go_sem, 1)

    send_forward(0)

    labels = lax.fori_loop(1, NG, lambda g, acc: acc + make_place(g), labels)
    lab_out[...] = labels

    def send_label(k):
        to = peer(k)
        pltpu.make_async_remote_copy(
            src_ref=lab_out.at[pl.ds(to, 1)], dst_ref=lab_in.at[pl.ds(me, 1)],
            send_sem=l_send, recv_sem=l_recv,
            device_id=(dp, to), device_id_type=MESH).start()

    loop(1, N_SEQ, send_label)
    lab_self = pltpu.make_async_copy(
        lab_out.at[pl.ds(me, 1)], lab_in.at[pl.ds(me, 1)], lab_self_sem)
    lab_self.start()

    def pack_send(g):
        pack(g)
        send_forward(g)

    loop(1, NG, pack_send)
    loop(0, NG, make_back)
    label_all().wait_recv()
    lab_self.wait()

    factor = HD ** (-0.5)

    def chip_copy(n):
        return pltpu.make_async_remote_copy(
            src_ref=gp.at[n], dst_ref=c_in.at[n], send_sem=c_send.at[n], recv_sem=c_recv.at[n],
            device_id=sibling, device_id_type=MESH)

    def gain_along(n):
        chip_copy(n).wait_recv()
        chip_sum[n] = gp[n] + c_in[n]
        z_in[n, dp] = chip_sum[n]

        def send(k):
            pltpu.make_async_remote_copy(
                src_ref=chip_sum.at[n], dst_ref=z_in.at[n, dp],
                send_sem=z_send.at[n], recv_sem=z_recv.at[n],
                device_id=((dp + k) % N_DP, me), device_id_type=MESH).start()

        loop(1, N_DP, send)

    def along_all(n):
        return pltpu.make_async_remote_copy(
            src_ref=z_in.at[n, pl.ds(0, N_DP - 1)], dst_ref=z_in.at[n, pl.ds(0, N_DP - 1)],
            send_sem=z_send.at[n], recv_sem=z_recv.at[n],
            device_id=sibling, device_id_type=MESH)

    def gain_plane(n):
        along_all(n).wait_recv()
        z_sum[n] = jnp.sum(z_in[n], axis=0)
        p_in[n, chip] = z_sum[n]

        def send(k):
            pltpu.make_async_remote_copy(
                src_ref=z_sum.at[n], dst_ref=p_in.at[n, chip],
                send_sem=p_send.at[n], recv_sem=p_recv.at[n],
                device_id=(dp, peer(k)), device_id_type=MESH).start()

        loop(1, N_SEQ, send)

    def plane_all(n, count):
        return pltpu.make_async_remote_copy(
            src_ref=p_in.at[n, pl.ds(0, count)], dst_ref=p_in.at[n, pl.ds(0, count)],
            send_sem=p_send.at[n], recv_sem=p_recv.at[n],
            device_id=sibling, device_id_type=MESH)

    def attend(g):
        @pl.when((g == 3) & (core == 1))
        def _():
            pl.semaphore_wait(barrier, N_DP - 1)
            gain_along(0)

        forward_all(g).wait_recv()
        pltpu.make_async_copy(outbox.at[g, me], inbox.at[g, me], self_sem.at[g]).wait()
        shape = (ROWS, HD)
        r = iota(shape, 0)
        head = head_of(shape, 0)
        gain_rows = jnp.zeros(shape, F32)
        for h in range(GH):
            gain_rows = jnp.where(head == h, gain_v[pl.ds(GH * g + h, 1), :], gain_rows)
        from_src = jnp.where(
            iota((ROWS, N_SEQ), 0) // MSG == iota((ROWS, N_SEQ), 1), 1.0, 0.0
        ).astype(BF16)
        arrived = dot(from_src, lab_in[...].astype(BF16))
        arrived = jnp.where(iota(shape, 1) == MSG * g + r % MSG, arrived, 0.0).astype(BF16)
        code_col = dot(arrived, jnp.ones((HD, HD), BF16)) + (2 * head).astype(F32)
        code_row = dot_nt(jnp.ones((8, HD), BF16), arrived)[0:1, :] + (
            2 * head_of((1, ROWS), 1)
        ).astype(F32)

        def part(t, lo, hi):
            n = hi - lo
            return inbox[g, lo // MSG : hi // MSG, :, t * HD : (t + 1) * HD].reshape(n, HD)

        query = part(0, 0, ROWS)
        raw = part(1, 0, ROWS).astype(F32)
        value = part(2, 0, ROWS)
        upstream = part(3, 0, ROWS)
        scaled = (raw * gain_rows).astype(BF16)
        for i in range(GH):
            lo, hi = i * 128, (i + 1) * 128
            scores = dot_nt(scaled[:hi], query[lo:hi]) * factor
            allowed = (code_col[:hi] == code_row[:, lo:hi]) & (
                iota((hi, 128), 0) <= iota((hi, 128), 1) + lo
            )
            scores = jnp.where(allowed, scores, NEG)
            expo = jnp.exp(scores - jnp.max(scores, axis=0, keepdims=True))
            weights = expo * (1.0 / jnp.sum(expo, axis=0, keepdims=True))
            rounded = weights.astype(BF16)
            rmat[:hi, lo:hi] = rounded
            inner = dot_nt(value[:hi], upstream[lo:hi])
            delta = jnp.sum(rounded.astype(F32) * inner, axis=0, keepdims=True)
            grad = (weights * (inner - delta)).astype(BF16)
            dmat[:hi, lo:hi] = grad
            query_grad = (dot_tn(grad, scaled[:hi]) * factor).astype(BF16)
            ret_out[g, lo // MSG : hi // MSG, :, 0:HD] = query_grad.reshape(
                128 // MSG, MSG, HD)
        total = jnp.zeros((MSG, HD), F32)
        for j in range(GH):
            lo, hi = j * 128, (j + 1) * 128
            value_grad = dot(rmat[lo:hi, lo:], upstream[lo:]).astype(BF16)
            ret_out[g, lo // MSG : hi // MSG, :, 2 * HD : 3 * HD] = value_grad.reshape(
                128 // MSG, MSG, HD)
            scaled_grad = (dot(dmat[lo:hi, lo:], query[lo:]) * factor).astype(BF16).astype(F32)
            key_grad = (gain_rows[lo:hi] * scaled_grad).astype(BF16)
            ret_out[g, lo // MSG : hi // MSG, :, HD : 2 * HD] = key_grad.reshape(
                128 // MSG, MSG, HD)
            total = total + jnp.sum((raw[lo:hi] * scaled_grad).reshape(128 // MSG, MSG, HD), axis=0)

        rows16 = iota((MSG, HD), 0) // MOST
        for h in range(GH):
            gp[g // 2, pl.ds(GH * (g % 2) + h, 1), :] = jnp.sum(
                jnp.where(rows16 == h, total, 0.0), axis=0, keepdims=True)

        @pl.when((g % 2 == 1) & (core == 0))
        def _():
            chip_copy(g // 2).start()

        @pl.when((g == 3) & (core == 1))
        def _():
            gain_along(1)

        def send_back(k):
            to = peer(k)
            pltpu.make_async_remote_copy(
                src_ref=ret_out.at[g, to], dst_ref=ret_in.at[g, me],
                send_sem=b_send.at[g], recv_sem=b_recv.at[g],
                device_id=(dp, to), device_id_type=MESH).start()

        loop(1, N_SEQ, send_back)
        pltpu.make_async_copy(ret_out.at[g, me], ret_in.at[g, me], ret_self_sem.at[g]).start()

    loop(0, NG, attend)

    def unpack(g):
        back_all(g).wait_recv()
        pltpu.make_async_copy(ret_out.at[g, me], ret_in.at[g, me], ret_self_sem.at[g]).wait()
        head = head_of((TOK, ROWS), 1)
        chosen = back_place[g]
        zero = jnp.zeros_like(chosen)
        left = jnp.concatenate([jnp.where(head == h, chosen, zero) for h in range(GH)], axis=0)
        home = dot(left, ret_in[g].reshape(ROWS, BACK)).astype(BF16)
        for t, ref in enumerate((dq_ref, dk_ref, dv_ref)):
            for h in range(GH):
                cols = pl.ds(pl.multiple_of((g * GH + h) * HD, HD), HD)
                ref[0, :, cols] = home[h * TOK : (h + 1) * TOK, t * HD : (t + 1) * HD]

    @pl.when(core == 1)
    def _():
        gain_plane(0)

    unpack(0)

    @pl.when(core == 1)
    def _():
        gain_plane(1)

    unpack(1)
    unpack(2)
    unpack(3)

    @pl.when(core == 0)
    def _():
        for n in range(2):
            plane_all(n, N_SEQ // 2).wait_recv()
            chip_copy(n).wait_send()

    @pl.when(core == 1)
    def _():
        for n in range(2):
            plane_all(n, N_SEQ // 2 - 1).wait_recv()
            along_all(n).wait_send()
            plane_all(n, N_SEQ // 2 - 1).wait_send()
            plane_all(n, N_SEQ // 2).wait_send()

    for n in range(2):
        gg_ref[n * 8 : (n + 1) * 8, :] = jnp.sum(p_in[n], axis=0)

    def finish(g):
        forward_all(g).wait_send()
        back_all(g).wait_send()

    loop(0, NG, finish)
    label_all().wait_send()


def hand_over(a, b, c, d, oa, ob, oc, od, sem):
    copies = [
        pltpu.make_async_copy(src, dst, sem.at[i])
        for i, (src, dst) in enumerate(zip((a, b, c, d), (oa, ob, oc, od)))
    ]
    for copy in copies:
        copy.start()
    for copy in copies:
        copy.wait()


def on_device(queries, keys, values, d_out, cluster_ids, gain):
    anywhere = pl.BlockSpec(memory_space=pl.ANY)
    in_vmem = pl.BlockSpec(memory_space=pltpu.VMEM)
    rows = jax.ShapeDtypeStruct(queries.shape, BF16)
    dma = pltpu.SemaphoreType.DMA
    query_grad, key_grad, value_grad, gain_grad = pl.pallas_call(
        kernel,
        out_shape=(rows, rows, rows, jax.ShapeDtypeStruct((H, HD), F32)),
        in_specs=[anywhere] * 5 + [in_vmem],
        out_specs=(in_vmem,) * 4,
        scratch_shapes=[
            pltpu.VMEM((NG, 4, TOK, GH * HD), BF16),
            pltpu.VMEM((H, TOK), jnp.int32),
            pltpu.VMEM((NG, ROWS, TOK), BF16),
            pltpu.VMEM((NG, TOK, ROWS), BF16),
            pltpu.VMEM((NG, N_SEQ, MSG, WIDE), BF16),
            pltpu.VMEM((NG, N_SEQ, MSG, WIDE), BF16),
            pltpu.VMEM((NG, N_SEQ, MSG, BACK), BF16),
            pltpu.VMEM((NG, N_SEQ, MSG, BACK), BF16),
            pltpu.VMEM((N_SEQ, HD), F32),
            pltpu.VMEM((N_SEQ, HD), F32),
            pltpu.VMEM((ROWS, ROWS), BF16),
            pltpu.VMEM((ROWS, ROWS), BF16),
            pltpu.VMEM((2, 8, HD), F32),
            pltpu.VMEM((2, 8, HD), F32),
            pltpu.VMEM((2, 8, HD), F32),
            pltpu.VMEM((2, N_DP, 8, HD), F32),
            pltpu.VMEM((2, 8, HD), F32),
            pltpu.VMEM((2, N_SEQ // 2, 8, HD), F32),
            dma((NG,)), dma, dma((NG,)), dma((NG,)), dma, pltpu.SemaphoreType.REGULAR,
            dma((NG,)), dma((NG,)), dma((NG,)), dma((NG,)), dma, dma,
            dma((2,)), dma((2,)), dma((2,)), dma((2,)), dma((2,)), dma((2,)),
        ],
        compiler_params=pltpu.CompilerParams(
            collective_id=0, has_side_effects=True, vmem_limit_bytes=52 * 2**20
        ),
    )(queries, keys, values, d_out, cluster_ids.swapaxes(1, 2), gain.reshape(H, HD))
    query_grad, key_grad, value_grad, gain_grad = pl.pallas_call(
        hand_over,
        out_shape=(rows, rows, rows, jax.ShapeDtypeStruct((H, HD), F32)),
        in_specs=[in_vmem] * 4,
        out_specs=(anywhere,) * 4,
        scratch_shapes=[dma((4,))],
        compiler_params=pltpu.CompilerParams(vmem_limit_bytes=4 * 2**20),
    )(query_grad, key_grad, value_grad, gain_grad)
    return query_grad, key_grad, value_grad, gain_grad.reshape(H * HD)


def solution(mesh):
    rows = P("dp", "seq", None)
    return jax.shard_map(
        on_device, mesh=mesh, in_specs=(rows,) * 5 + (P(),),
        out_specs=(rows, rows, rows, P()), check_vma=False,
    )
```

```python
import jax
import jax.numpy as jnp
from jax import lax
from jax.experimental import pallas as pl
from jax.experimental.pallas import tpu as pltpu
from jax.sharding import PartitionSpec as P

H = 16
HD = 128
CPO = 2
MOST = 4
TOK = 128
N_SEQ = 32
N_DP = 16
GH = 4
NG = H // GH
ROWS = N_SEQ * GH * MOST
MSG = GH * MOST
WIDE = 4 * HD
BACK = 3 * HD
MESH = pl.DeviceIdType.MESH
F32 = jnp.float32
BF16 = jnp.bfloat16
NEG = -1e30


def iota(shape, dim):
    return lax.broadcasted_iota(jnp.int32, shape, dim)


def dot(a, b):
    return lax.dot_general(a, b, (((1,), (0,)), ((), ())), preferred_element_type=F32)


def dot_nt(a, b):
    return lax.dot_general(a, b, (((1,), (1,)), ((), ())), preferred_element_type=F32)


def dot_tn(a, b):
    return lax.dot_general(a, b, (((0,), (0,)), ((), ())), preferred_element_type=F32)


def kernel(
    q_hbm, k_hbm, v_hbm, d_hbm, cid_hbm, gain_v,
    dq_ref, dk_ref, dv_ref, gg_ref,
    xin, cid_v, place, back_place, outbox, inbox, ret_out, ret_in,
    lab_out, lab_in, rmat, dmat,
    gp, c_in, chip_sum, z_in, z_sum, p_in,
    in_sem, small_sem, self_sem, ret_self_sem, lab_self_sem, go_sem,
    f_send, f_recv, b_send, b_recv, l_send, l_recv,
    c_send, c_recv, z_send, z_recv, p_send, p_recv,
):
    me = lax.axis_index("seq")
    dp = lax.axis_index("dp")
    core = me % 2
    my = (me // 2) % 4
    mx = me // 8
    chip = me // 2

    def peer(k):
        dx, dy, dc = k // 8, (k // 2) % 4, k % 2
        return ((mx + dx) % 4) * 8 + ((my + dy) % 4) * 2 + (core + dc) % 2

    def loop(lo, hi, body):
        def step(i, carry):
            body(i)
            return carry

        lax.fori_loop(lo, hi, step, 0)

    barrier = pltpu.get_barrier_semaphore()
    sibling = (dp, chip * 2 + 1 - core)

    def greet_plane(c):
        @pl.when(2 * c != me)
        def _():
            pl.semaphore_signal(barrier, inc=1, device_id=(dp, 2 * c), device_id_type=MESH)

    loop(0, N_SEQ // 2, greet_plane)

    @pl.when(core == 1)
    def _():
        loop(1, N_DP, lambda k: pl.semaphore_signal(
            barrier, inc=1, device_id=((dp + k) % N_DP, me), device_id_type=MESH))

    cid_copy = pltpu.make_async_copy(cid_hbm.at[0], cid_v, small_sem)
    cid_copy.start()

    def load(g):
        cols = pl.ds(pl.multiple_of(g * GH * HD, GH * HD), GH * HD)
        for t, ref in enumerate((q_hbm, k_hbm, v_hbm, d_hbm)):
            pltpu.make_async_copy(ref.at[0, :, cols], xin.at[g, t], in_sem.at[g]).start()

    loop(0, NG, load)
    cid_copy.wait()
    cid = cid_v[...].astype(F32).astype(BF16)

    def select(g):
        r = iota((ROWS, H), 0)
        return jnp.where(iota((ROWS, H), 1) == GH * g + (r // MOST) % GH, 1.0, 0.0).astype(BF16)

    def select_back(g):
        r = iota((H, ROWS), 1)
        return jnp.where(iota((H, ROWS), 0) == GH * g + (r // MOST) % GH, 1.0, 0.0).astype(BF16)

    def head_of(shape, dim):
        return (iota(shape, dim) // MOST) % GH

    def make_place(g):
        shape = (ROWS, TOK)
        r = iota(shape, 0)
        label = dot(select(g), cid) - (CPO * (r // MSG)).astype(F32)
        member = (label == 0.0) | (label == 1.0)
        before = jnp.where(iota((TOK, TOK), 0) < iota((TOK, TOK), 1), 1.0, 0.0).astype(BF16)
        rank = dot(jnp.where(member, 1.0, 0.0).astype(BF16), before)
        chosen = member & (rank == (r % MOST).astype(F32))
        place[g] = jnp.where(chosen, 1.0, 0.0).astype(BF16)
        row_label = dot(
            jnp.where(chosen, label, 0.0).astype(BF16), jnp.ones((TOK, TOK), BF16)
        )
        spread = jnp.where(iota(shape, 1) == MSG * g + r % MSG, row_label, 0.0).astype(BF16)
        owners = jnp.where(
            iota((N_SEQ, ROWS), 1) // MSG == iota((N_SEQ, ROWS), 0), 1.0, 0.0
        ).astype(BF16)
        return dot(owners, spread)

    def make_back(g):
        shape = (TOK, ROWS)
        r = iota(shape, 1)
        label = dot_tn(cid, select_back(g)) - (CPO * (r // MSG)).astype(F32)
        member = (label == 0.0) | (label == 1.0)
        before = jnp.where(iota((TOK, TOK), 1) < iota((TOK, TOK), 0), 1.0, 0.0).astype(BF16)
        rank = dot(before, jnp.where(member, 1.0, 0.0).astype(BF16))
        chosen = member & (rank == (r % MOST).astype(F32))
        back_place[g] = jnp.where(chosen, 1.0, 0.0).astype(BF16)

    def pack(g):
        pltpu.make_async_copy(xin.at[g], xin.at[g], in_sem.at[g]).wait()
        head = head_of((ROWS, TOK), 0)
        chosen = place[g]
        zero = jnp.zeros_like(chosen)
        left = jnp.concatenate([jnp.where(head == h, chosen, zero) for h in range(GH)], axis=1)
        for t in range(4):
            stack = jnp.concatenate(
                [xin[g, t, :, h * HD : (h + 1) * HD] for h in range(GH)], axis=0
            )
            outbox[g, :, :, t * HD : (t + 1) * HD] = (
                dot(left, stack).astype(BF16).reshape(N_SEQ, MSG, HD)
            )

    def forward(g, k):
        to = peer(k)
        return pltpu.make_async_remote_copy(
            src_ref=outbox.at[g, to], dst_ref=inbox.at[g, me],
            send_sem=f_send.at[g], recv_sem=f_recv.at[g],
            device_id=(dp, to), device_id_type=MESH)

    def send_forward(g):
        loop(1, N_SEQ, lambda k: forward(g, k).start())
        pltpu.make_async_copy(outbox.at[g, me], inbox.at[g, me], self_sem.at[g]).start()

    def forward_all(g):
        return pltpu.make_async_remote_copy(
            src_ref=outbox.at[g, pl.ds(0, N_SEQ - 1)], dst_ref=inbox.at[g, pl.ds(0, N_SEQ - 1)],
            send_sem=f_send.at[g], recv_sem=f_recv.at[g],
            device_id=(dp, peer(1)), device_id_type=MESH)

    def back_all(g):
        return pltpu.make_async_remote_copy(
            src_ref=ret_out.at[g, pl.ds(0, N_SEQ - 1)], dst_ref=ret_in.at[g, pl.ds(0, N_SEQ - 1)],
            send_sem=b_send.at[g], recv_sem=b_recv.at[g],
            device_id=(dp, peer(1)), device_id_type=MESH)

    def label_all():
        return pltpu.make_async_remote_copy(
            src_ref=lab_out.at[pl.ds(0, N_SEQ - 1)], dst_ref=lab_in.at[pl.ds(0, N_SEQ - 1)],
            send_sem=l_send, recv_sem=l_recv,
            device_id=(dp, peer(1)), device_id_type=MESH)

    labels = make_place(0)
    pack(0)

    @pl.when(core == 0)
    def _():
        pl.semaphore_wait(barrier, N_SEQ - 1)
        pl.semaphore_signal(go_sem, inc=1, device_id=sibling, device_id_type=MESH)

    @pl.when(core == 1)
    def _():
        pl.semaphore_wait(go_sem, 1)

    send_forward(0)

    labels = lax.fori_loop(1, NG, lambda g, acc: acc + make_place(g), labels)
    lab_out[...] = labels

    def send_label(k):
        to = peer(k)
        pltpu.make_async_remote_copy(
            src_ref=lab_out.at[pl.ds(to, 1)], dst_ref=lab_in.at[pl.ds(me, 1)],
            send_sem=l_send, recv_sem=l_recv,
            device_id=(dp, to), device_id_type=MESH).start()

    loop(1, N_SEQ, send_label)
    lab_self = pltpu.make_async_copy(
        lab_out.at[pl.ds(me, 1)], lab_in.at[pl.ds(me, 1)], lab_self_sem)
    lab_self.start()

    def pack_send(g):
        pack(g)
        send_forward(g)

    loop(1, NG, pack_send)
    loop(0, NG, make_back)
    label_all().wait_recv()
    lab_self.wait()

    factor = HD ** (-0.5)

    def chip_copy(n):
        return pltpu.make_async_remote_copy(
            src_ref=gp.at[n], dst_ref=c_in.at[n], send_sem=c_send.at[n], recv_sem=c_recv.at[n],
            device_id=sibling, device_id_type=MESH)

    def gain_along(n):
        chip_copy(n).wait_recv()
        chip_sum[n] = gp[n] + c_in[n]
        z_in[n, dp] = chip_sum[n]

        def send(k):
            pltpu.make_async_remote_copy(
                src_ref=chip_sum.at[n], dst_ref=z_in.at[n, dp],
                send_sem=z_send.at[n], recv_sem=z_recv.at[n],
                device_id=((dp + k) % N_DP, me), device_id_type=MESH).start()

        loop(1, N_DP, send)

    def along_all(n):
        return pltpu.make_async_remote_copy(
            src_ref=z_in.at[n, pl.ds(0, N_DP - 1)], dst_ref=z_in.at[n, pl.ds(0, N_DP - 1)],
            send_sem=z_send.at[n], recv_sem=z_recv.at[n],
            device_id=sibling, device_id_type=MESH)

    def gain_plane(n):
        along_all(n).wait_recv()
        z_sum[n] = jnp.sum(z_in[n], axis=0)
        p_in[n, chip] = z_sum[n]

        def send(k):
            pltpu.make_async_remote_copy(
                src_ref=z_sum.at[n], dst_ref=p_in.at[n, chip],
                send_sem=p_send.at[n], recv_sem=p_recv.at[n],
                device_id=(dp, peer(k)), device_id_type=MESH).start()

        loop(1, N_SEQ, send)

    def plane_all(n, count):
        return pltpu.make_async_remote_copy(
            src_ref=p_in.at[n, pl.ds(0, count)], dst_ref=p_in.at[n, pl.ds(0, count)],
            send_sem=p_send.at[n], recv_sem=p_recv.at[n],
            device_id=sibling, device_id_type=MESH)

    def attend(g):
        @pl.when((g == 3) & (core == 1))
        def _():
            pl.semaphore_wait(barrier, N_DP - 1)
            gain_along(0)

        forward_all(g).wait_recv()
        pltpu.make_async_copy(outbox.at[g, me], inbox.at[g, me], self_sem.at[g]).wait()
        shape = (ROWS, HD)
        r = iota(shape, 0)
        head = head_of(shape, 0)
        gain_rows = jnp.zeros(shape, F32)
        for h in range(GH):
            gain_rows = jnp.where(head == h, gain_v[pl.ds(GH * g + h, 1), :], gain_rows)
        from_src = jnp.where(
            iota((ROWS, N_SEQ), 0) // MSG == iota((ROWS, N_SEQ), 1), 1.0, 0.0
        ).astype(BF16)
        arrived = dot(from_src, lab_in[...].astype(BF16))
        arrived = jnp.where(iota(shape, 1) == MSG * g + r % MSG, arrived, 0.0).astype(BF16)
        code_col = dot(arrived, jnp.ones((HD, HD), BF16)) + (2 * head).astype(F32)
        code_row = dot_nt(jnp.ones((8, HD), BF16), arrived)[0:1, :] + (
            2 * head_of((1, ROWS), 1)
        ).astype(F32)

        def part(t, lo, hi):
            n = hi - lo
            return inbox[g, lo // MSG : hi // MSG, :, t * HD : (t + 1) * HD].reshape(n, HD)

        query = part(0, 0, ROWS)
        raw = part(1, 0, ROWS).astype(F32)
        value = part(2, 0, ROWS)
        upstream = part(3, 0, ROWS)
        scaled = (raw * gain_rows).astype(BF16)
        for i in range(GH):
            lo, hi = i * 128, (i + 1) * 128
            scores = dot_nt(scaled[:hi], query[lo:hi]) * factor
            allowed = (code_col[:hi] == code_row[:, lo:hi]) & (
                iota((hi, 128), 0) <= iota((hi, 128), 1) + lo
            )
            scores = jnp.where(allowed, scores, NEG)
            expo = jnp.exp(scores - jnp.max(scores, axis=0, keepdims=True))
            weights = expo * (1.0 / jnp.sum(expo, axis=0, keepdims=True))
            rounded = weights.astype(BF16)
            rmat[:hi, lo:hi] = rounded
            inner = dot_nt(value[:hi], upstream[lo:hi])
            delta = jnp.sum(rounded.astype(F32) * inner, axis=0, keepdims=True)
            grad = (weights * (inner - delta)).astype(BF16)
            dmat[:hi, lo:hi] = grad
            query_grad = (dot_tn(grad, scaled[:hi]) * factor).astype(BF16)
            ret_out[g, lo // MSG : hi // MSG, :, 0:HD] = query_grad.reshape(
                128 // MSG, MSG, HD)
        total = jnp.zeros((MSG, HD), F32)
        for j in range(GH):
            lo, hi = j * 128, (j + 1) * 128
            value_grad = dot(rmat[lo:hi, lo:], upstream[lo:]).astype(BF16)
            ret_out[g, lo // MSG : hi // MSG, :, 2 * HD : 3 * HD] = value_grad.reshape(
                128 // MSG, MSG, HD)
            scaled_grad = (dot(dmat[lo:hi, lo:], query[lo:]) * factor).astype(BF16).astype(F32)
            key_grad = (gain_rows[lo:hi] * scaled_grad).astype(BF16)
            ret_out[g, lo // MSG : hi // MSG, :, HD : 2 * HD] = key_grad.reshape(
                128 // MSG, MSG, HD)
            total = total + jnp.sum((raw[lo:hi] * scaled_grad).reshape(128 // MSG, MSG, HD), axis=0)

        rows16 = iota((MSG, HD), 0) // MOST
        for h in range(GH):
            gp[g // 2, pl.ds(GH * (g % 2) + h, 1), :] = jnp.sum(
                jnp.where(rows16 == h, total, 0.0), axis=0, keepdims=True)

        @pl.when((g % 2 == 1) & (core == 0))
        def _():
            chip_copy(g // 2).start()

        @pl.when((g == 3) & (core == 1))
        def _():
            gain_along(1)

        def send_back(k):
            to = peer(k)
            pltpu.make_async_remote_copy(
                src_ref=ret_out.at[g, to], dst_ref=ret_in.at[g, me],
                send_sem=b_send.at[g], recv_sem=b_recv.at[g],
                device_id=(dp, to), device_id_type=MESH).start()

        loop(1, N_SEQ, send_back)
        pltpu.make_async_copy(ret_out.at[g, me], ret_in.at[g, me], ret_self_sem.at[g]).start()

    loop(0, NG, attend)

    def unpack(g):
        back_all(g).wait_recv()
        pltpu.make_async_copy(ret_out.at[g, me], ret_in.at[g, me], ret_self_sem.at[g]).wait()
        head = head_of((TOK, ROWS), 1)
        chosen = back_place[g]
        zero = jnp.zeros_like(chosen)
        left = jnp.concatenate([jnp.where(head == h, chosen, zero) for h in range(GH)], axis=0)
        home = dot(left, ret_in[g].reshape(ROWS, BACK)).astype(BF16)
        for t, ref in enumerate((dq_ref, dk_ref, dv_ref)):
            for h in range(GH):
                cols = pl.ds(pl.multiple_of((g * GH + h) * HD, HD), HD)
                ref[0, :, cols] = home[h * TOK : (h + 1) * TOK, t * HD : (t + 1) * HD]

    @pl.when(core == 1)
    def _():
        gain_plane(0)

    unpack(0)

    @pl.when(core == 1)
    def _():
        gain_plane(1)

    unpack(1)
    unpack(2)
    unpack(3)

    @pl.when(core == 0)
    def _():
        for n in range(2):
            plane_all(n, N_SEQ // 2).wait_recv()
            chip_copy(n).wait_send()

    @pl.when(core == 1)
    def _():
        for n in range(2):
            plane_all(n, N_SEQ // 2 - 1).wait_recv()
            along_all(n).wait_send()
            plane_all(n, N_SEQ // 2 - 1).wait_send()
            plane_all(n, N_SEQ // 2).wait_send()

    for n in range(2):
        gg_ref[n * 8 : (n + 1) * 8, :] = jnp.sum(p_in[n], axis=0)

    def finish(g):
        forward_all(g).wait_send()
        back_all(g).wait_send()

    loop(0, NG, finish)
    label_all().wait_send()


def hand_over(a, b, c, d, oa, ob, oc, od, sem):
    copies = [
        pltpu.make_async_copy(src, dst, sem.at[i])
        for i, (src, dst) in enumerate(zip((a, b, c, d), (oa, ob, oc, od)))
    ]
    for copy in copies:
        copy.start()
    for copy in copies:
        copy.wait()


def on_device(queries, keys, values, d_out, cluster_ids, gain):
    anywhere = pl.BlockSpec(memory_space=pl.ANY)
    in_vmem = pl.BlockSpec(memory_space=pltpu.VMEM)
    rows = jax.ShapeDtypeStruct(queries.shape, BF16)
    dma = pltpu.SemaphoreType.DMA
    query_grad, key_grad, value_grad, gain_grad = pl.pallas_call(
        kernel,
        out_shape=(rows, rows, rows, jax.ShapeDtypeStruct((H, HD), F32)),
        in_specs=[anywhere] * 4 + [pl.BlockSpec(memory_space=pltpu.HBM), in_vmem],
        out_specs=(in_vmem,) * 4,
        scratch_shapes=[
            pltpu.VMEM((NG, 4, TOK, GH * HD), BF16),
            pltpu.VMEM((H, TOK), jnp.int32),
            pltpu.VMEM((NG, ROWS, TOK), BF16),
            pltpu.VMEM((NG, TOK, ROWS), BF16),
            pltpu.VMEM((NG, N_SEQ, MSG, WIDE), BF16),
            pltpu.VMEM((NG, N_SEQ, MSG, WIDE), BF16),
            pltpu.VMEM((NG, N_SEQ, MSG, BACK), BF16),
            pltpu.VMEM((NG, N_SEQ, MSG, BACK), BF16),
            pltpu.VMEM((N_SEQ, HD), F32),
            pltpu.VMEM((N_SEQ, HD), F32),
            pltpu.VMEM((ROWS, ROWS), BF16),
            pltpu.VMEM((ROWS, ROWS), BF16),
            pltpu.VMEM((2, 8, HD), F32),
            pltpu.VMEM((2, 8, HD), F32),
            pltpu.VMEM((2, 8, HD), F32),
            pltpu.VMEM((2, N_DP, 8, HD), F32),
            pltpu.VMEM((2, 8, HD), F32),
            pltpu.VMEM((2, N_SEQ // 2, 8, HD), F32),
            dma((NG,)), dma, dma((NG,)), dma((NG,)), dma, pltpu.SemaphoreType.REGULAR,
            dma((NG,)), dma((NG,)), dma((NG,)), dma((NG,)), dma, dma,
            dma((2,)), dma((2,)), dma((2,)), dma((2,)), dma((2,)), dma((2,)),
        ],
        compiler_params=pltpu.CompilerParams(
            collective_id=0, has_side_effects=True, vmem_limit_bytes=52 * 2**20
        ),
    )(queries, keys, values, d_out, pltpu.with_memory_space_constraint(cluster_ids.swapaxes(1, 2), pltpu.HBM), pltpu.with_memory_space_constraint(gain.reshape(H, HD), pltpu.HBM))
    query_grad, key_grad, value_grad, gain_grad = pl.pallas_call(
        hand_over,
        out_shape=(rows, rows, rows, jax.ShapeDtypeStruct((H, HD), F32)),
        in_specs=[in_vmem] * 4,
        out_specs=(anywhere,) * 4,
        scratch_shapes=[dma((4,))],
        compiler_params=pltpu.CompilerParams(vmem_limit_bytes=4 * 2**20),
    )(query_grad, key_grad, value_grad, gain_grad)
    return query_grad, key_grad, value_grad, gain_grad.reshape(H * HD)


def solution(mesh):
    rows = P("dp", "seq", None)
    return jax.shard_map(
        on_device, mesh=mesh, in_specs=(rows,) * 5 + (P(),),
        out_specs=(rows, rows, rows, P()), check_vma=False,
    )
```

```python
import jax
import jax.numpy as jnp
from jax import lax
from jax.experimental import pallas as pl
from jax.experimental.pallas import tpu as pltpu
from jax.sharding import PartitionSpec as P

H = 16
HD = 128
CPO = 2
MOST = 4
TOK = 128
N_SEQ = 32
N_DP = 16
GH = 4
NG = H // GH
ROWS = N_SEQ * GH * MOST
MSG = GH * MOST
WIDE = 4 * HD
BACK = 3 * HD
MESH = pl.DeviceIdType.MESH
F32 = jnp.float32
BF16 = jnp.bfloat16
NEG = -1e30


def iota(shape, dim):
    return lax.broadcasted_iota(jnp.int32, shape, dim)


def dot(a, b):
    return lax.dot_general(a, b, (((1,), (0,)), ((), ())), preferred_element_type=F32)


def dot_nt(a, b):
    return lax.dot_general(a, b, (((1,), (1,)), ((), ())), preferred_element_type=F32)


def dot_tn(a, b):
    return lax.dot_general(a, b, (((0,), (0,)), ((), ())), preferred_element_type=F32)


def kernel(
    q_hbm, k_hbm, v_hbm, d_hbm, cid_hbm, gain_v,
    dq_ref, dk_ref, dv_ref, gg_ref,
    xin, cid_v, place, back_place, outbox, inbox, ret_out, ret_in,
    lab_out, lab_in, rmat, dmat,
    gp, c_in, chip_sum, z_in, z_sum, p_in,
    in_sem, small_sem, self_sem, ret_self_sem, lab_self_sem, go_sem,
    f_send, f_recv, b_send, b_recv, l_send, l_recv,
    c_send, c_recv, z_send, z_recv, p_send, p_recv,
):
    me = lax.axis_index("seq")
    dp = lax.axis_index("dp")
    core = me % 2
    my = (me // 2) % 4
    mx = me // 8
    chip = me // 2

    def peer(k):
        dx, dy, dc = k // 8, (k // 2) % 4, k % 2
        return ((mx + dx) % 4) * 8 + ((my + dy) % 4) * 2 + (core + dc) % 2

    def loop(lo, hi, body):
        def step(i, carry):
            body(i)
            return carry

        lax.fori_loop(lo, hi, step, 0)

    barrier = pltpu.get_barrier_semaphore()
    sibling = (dp, chip * 2 + 1 - core)

    def greet_plane(c):
        @pl.when(2 * c != me)
        def _():
            pl.semaphore_signal(barrier, inc=1, device_id=(dp, 2 * c), device_id_type=MESH)

    loop(0, N_SEQ // 2, greet_plane)

    @pl.when(core == 1)
    def _():
        loop(1, N_DP, lambda k: pl.semaphore_signal(
            barrier, inc=1, device_id=((dp + k) % N_DP, me), device_id_type=MESH))

    cid_copy = pltpu.make_async_copy(cid_hbm.at[0], cid_v, small_sem)
    cid_copy.start()

    def load(g):
        cols = pl.ds(pl.multiple_of(g * GH * HD, GH * HD), GH * HD)
        for t, ref in enumerate((q_hbm, k_hbm, v_hbm, d_hbm)):
            pltpu.make_async_copy(ref.at[0, :, cols], xin.at[g, t], in_sem.at[g]).start()

    loop(0, NG, load)
    cid_copy.wait()
    cid = cid_v[...].astype(F32).astype(BF16)

    def select(g):
        r = iota((ROWS, H), 0)
        return jnp.where(iota((ROWS, H), 1) == GH * g + (r // MOST) % GH, 1.0, 0.0).astype(BF16)

    def select_back(g):
        r = iota((H, ROWS), 1)
        return jnp.where(iota((H, ROWS), 0) == GH * g + (r // MOST) % GH, 1.0, 0.0).astype(BF16)

    def head_of(shape, dim):
        return (iota(shape, dim) // MOST) % GH

    def make_place(g):
        shape = (ROWS, TOK)
        r = iota(shape, 0)
        label = dot(select(g), cid) - (CPO * (r // MSG)).astype(F32)
        member = (label == 0.0) | (label == 1.0)
        before = jnp.where(iota((TOK, TOK), 0) < iota((TOK, TOK), 1), 1.0, 0.0).astype(BF16)
        rank = dot(jnp.where(member, 1.0, 0.0).astype(BF16), before)
        chosen = member & (rank == (r % MOST).astype(F32))
        place[g] = jnp.where(chosen, 1.0, 0.0).astype(BF16)
        row_label = dot(
            jnp.where(chosen, label, 0.0).astype(BF16), jnp.ones((TOK, TOK), BF16)
        )
        spread = jnp.where(iota(shape, 1) == MSG * g + r % MSG, row_label, 0.0).astype(BF16)
        owners = jnp.where(
            iota((N_SEQ, ROWS), 1) // MSG == iota((N_SEQ, ROWS), 0), 1.0, 0.0
        ).astype(BF16)
        return dot(owners, spread)

    def make_back(g):
        shape = (TOK, ROWS)
        r = iota(shape, 1)
        label = dot_tn(cid, select_back(g)) - (CPO * (r // MSG)).astype(F32)
        member = (label == 0.0) | (label == 1.0)
        before = jnp.where(iota((TOK, TOK), 1) < iota((TOK, TOK), 0), 1.0, 0.0).astype(BF16)
        rank = dot(before, jnp.where(member, 1.0, 0.0).astype(BF16))
        chosen = member & (rank == (r % MOST).astype(F32))
        back_place[g] = jnp.where(chosen, 1.0, 0.0).astype(BF16)

    def pack(g):
        pltpu.make_async_copy(xin.at[g], xin.at[g], in_sem.at[g]).wait()
        head = head_of((ROWS, TOK), 0)
        chosen = place[g]
        zero = jnp.zeros_like(chosen)
        left = jnp.concatenate([jnp.where(head == h, chosen, zero) for h in range(GH)], axis=1)
        for t in range(4):
            stack = jnp.concatenate(
                [xin[g, t, :, h * HD : (h + 1) * HD] for h in range(GH)], axis=0
            )
            outbox[g, :, :, t * HD : (t + 1) * HD] = (
                dot(left, stack).astype(BF16).reshape(N_SEQ, MSG, HD)
            )

    def forward(g, k):
        to = peer(k)
        return pltpu.make_async_remote_copy(
            src_ref=outbox.at[g, to], dst_ref=inbox.at[g, me],
            send_sem=f_send.at[g], recv_sem=f_recv.at[g],
            device_id=(dp, to), device_id_type=MESH)

    def send_forward(g):
        loop(1, N_SEQ, lambda k: forward(g, k).start())
        pltpu.make_async_copy(outbox.at[g, me], inbox.at[g, me], self_sem.at[g]).start()

    def forward_all(g):
        return pltpu.make_async_remote_copy(
            src_ref=outbox.at[g, pl.ds(0, N_SEQ - 1)], dst_ref=inbox.at[g, pl.ds(0, N_SEQ - 1)],
            send_sem=f_send.at[g], recv_sem=f_recv.at[g],
            device_id=(dp, peer(1)), device_id_type=MESH)

    def back_all(g):
        return pltpu.make_async_remote_copy(
            src_ref=ret_out.at[g, pl.ds(0, N_SEQ - 1)], dst_ref=ret_in.at[g, pl.ds(0, N_SEQ - 1)],
            send_sem=b_send.at[g], recv_sem=b_recv.at[g],
            device_id=(dp, peer(1)), device_id_type=MESH)

    def label_all():
        return pltpu.make_async_remote_copy(
            src_ref=lab_out.at[pl.ds(0, N_SEQ - 1)], dst_ref=lab_in.at[pl.ds(0, N_SEQ - 1)],
            send_sem=l_send, recv_sem=l_recv,
            device_id=(dp, peer(1)), device_id_type=MESH)

    labels = make_place(0)
    pack(0)

    @pl.when(core == 0)
    def _():
        pl.semaphore_wait(barrier, N_SEQ - 1)
        pl.semaphore_signal(go_sem, inc=1, device_id=sibling, device_id_type=MESH)

    @pl.when(core == 1)
    def _():
        pl.semaphore_wait(go_sem, 1)

    send_forward(0)

    labels = lax.fori_loop(1, NG, lambda g, acc: acc + make_place(g), labels)
    lab_out[...] = labels

    def send_label(k):
        to = peer(k)
        pltpu.make_async_remote_copy(
            src_ref=lab_out.at[pl.ds(to, 1)], dst_ref=lab_in.at[pl.ds(me, 1)],
            send_sem=l_send, recv_sem=l_recv,
            device_id=(dp, to), device_id_type=MESH).start()

    loop(1, N_SEQ, send_label)
    lab_self = pltpu.make_async_copy(
        lab_out.at[pl.ds(me, 1)], lab_in.at[pl.ds(me, 1)], lab_self_sem)
    lab_self.start()

    def pack_send(g):
        pack(g)
        send_forward(g)

    loop(1, NG, pack_send)
    loop(0, NG, make_back)
    label_all().wait_recv()
    lab_self.wait()

    factor = HD ** (-0.5)

    def chip_copy(n):
        return pltpu.make_async_remote_copy(
            src_ref=gp.at[n], dst_ref=c_in.at[n], send_sem=c_send.at[n], recv_sem=c_recv.at[n],
            device_id=sibling, device_id_type=MESH)

    def gain_along(n):
        chip_copy(n).wait_recv()
        chip_sum[n] = gp[n] + c_in[n]
        z_in[n, dp] = chip_sum[n]

        def send(k):
            pltpu.make_async_remote_copy(
                src_ref=chip_sum.at[n], dst_ref=z_in.at[n, dp],
                send_sem=z_send.at[n], recv_sem=z_recv.at[n],
                device_id=((dp + k) % N_DP, me), device_id_type=MESH).start()

        loop(1, N_DP, send)

    def along_all(n):
        return pltpu.make_async_remote_copy(
            src_ref=z_in.at[n, pl.ds(0, N_DP - 1)], dst_ref=z_in.at[n, pl.ds(0, N_DP - 1)],
            send_sem=z_send.at[n], recv_sem=z_recv.at[n],
            device_id=sibling, device_id_type=MESH)

    def gain_plane(n):
        along_all(n).wait_recv()
        z_sum[n] = jnp.sum(z_in[n], axis=0)
        p_in[n, chip] = z_sum[n]

        def send(k):
            pltpu.make_async_remote_copy(
                src_ref=z_sum.at[n], dst_ref=p_in.at[n, chip],
                send_sem=p_send.at[n], recv_sem=p_recv.at[n],
                device_id=(dp, peer(k)), device_id_type=MESH).start()

        loop(1, N_SEQ, send)

    def plane_all(n, count):
        return pltpu.make_async_remote_copy(
            src_ref=p_in.at[n, pl.ds(0, count)], dst_ref=p_in.at[n, pl.ds(0, count)],
            send_sem=p_send.at[n], recv_sem=p_recv.at[n],
            device_id=sibling, device_id_type=MESH)

    def attend(g):
        @pl.when((g == 2) & (core == 1))
        def _():
            pl.semaphore_wait(barrier, N_DP - 1)
            gain_along(0)

        @pl.when((g == 3) & (core == 1))
        def _():
            gain_plane(0)

        forward_all(g).wait_recv()
        pltpu.make_async_copy(outbox.at[g, me], inbox.at[g, me], self_sem.at[g]).wait()
        shape = (ROWS, HD)
        r = iota(shape, 0)
        head = head_of(shape, 0)
        gain_rows = jnp.zeros(shape, F32)
        for h in range(GH):
            gain_rows = jnp.where(head == h, gain_v[pl.ds(GH * g + h, 1), :], gain_rows)
        from_src = jnp.where(
            iota((ROWS, N_SEQ), 0) // MSG == iota((ROWS, N_SEQ), 1), 1.0, 0.0
        ).astype(BF16)
        arrived = dot(from_src, lab_in[...].astype(BF16))
        arrived = jnp.where(iota(shape, 1) == MSG * g + r % MSG, arrived, 0.0).astype(BF16)
        code_col = dot(arrived, jnp.ones((HD, HD), BF16)) + (2 * head).astype(F32)
        code_row = dot_nt(jnp.ones((8, HD), BF16), arrived)[0:1, :] + (
            2 * head_of((1, ROWS), 1)
        ).astype(F32)

        def part(t, lo, hi):
            n = hi - lo
            return inbox[g, lo // MSG : hi // MSG, :, t * HD : (t + 1) * HD].reshape(n, HD)

        query = part(0, 0, ROWS)
        raw = part(1, 0, ROWS).astype(F32)
        value = part(2, 0, ROWS)
        upstream = part(3, 0, ROWS)
        scaled = (raw * gain_rows).astype(BF16)
        for i in range(GH):
            lo, hi = i * 128, (i + 1) * 128
            scores = dot_nt(scaled[:hi], query[lo:hi]) * factor
            allowed = (code_col[:hi] == code_row[:, lo:hi]) & (
                iota((hi, 128), 0) <= iota((hi, 128), 1) + lo
            )
            scores = jnp.where(allowed, scores, NEG)
            expo = jnp.exp(scores - jnp.max(scores, axis=0, keepdims=True))
            weights = expo * (1.0 / jnp.sum(expo, axis=0, keepdims=True))
            rounded = weights.astype(BF16)
            rmat[:hi, lo:hi] = rounded
            inner = dot_nt(value[:hi], upstream[lo:hi])
            delta = jnp.sum(rounded.astype(F32) * inner, axis=0, keepdims=True)
            grad = (weights * (inner - delta)).astype(BF16)
            dmat[:hi, lo:hi] = grad
            query_grad = (dot_tn(grad, scaled[:hi]) * factor).astype(BF16)
            ret_out[g, lo // MSG : hi // MSG, :, 0:HD] = query_grad.reshape(
                128 // MSG, MSG, HD)
        total = jnp.zeros((MSG, HD), F32)
        for j in range(GH):
            lo, hi = j * 128, (j + 1) * 128
            value_grad = dot(rmat[lo:hi, lo:], upstream[lo:]).astype(BF16)
            ret_out[g, lo // MSG : hi // MSG, :, 2 * HD : 3 * HD] = value_grad.reshape(
                128 // MSG, MSG, HD)
            scaled_grad = (dot(dmat[lo:hi, lo:], query[lo:]) * factor).astype(BF16).astype(F32)
            key_grad = (gain_rows[lo:hi] * scaled_grad).astype(BF16)
            ret_out[g, lo // MSG : hi // MSG, :, HD : 2 * HD] = key_grad.reshape(
                128 // MSG, MSG, HD)
            total = total + jnp.sum((raw[lo:hi] * scaled_grad).reshape(128 // MSG, MSG, HD), axis=0)

        rows16 = iota((MSG, HD), 0) // MOST
        for h in range(GH):
            gp[g // 2, pl.ds(GH * (g % 2) + h, 1), :] = jnp.sum(
                jnp.where(rows16 == h, total, 0.0), axis=0, keepdims=True)

        @pl.when((g % 2 == 1) & (core == 0))
        def _():
            chip_copy(g // 2).start()

        @pl.when((g == 3) & (core == 1))
        def _():
            gain_along(1)

        def send_back(k):
            to = peer(k)
            pltpu.make_async_remote_copy(
                src_ref=ret_out.at[g, to], dst_ref=ret_in.at[g, me],
                send_sem=b_send.at[g], recv_sem=b_recv.at[g],
                device_id=(dp, to), device_id_type=MESH).start()

        loop(1, N_SEQ, send_back)
        pltpu.make_async_copy(ret_out.at[g, me], ret_in.at[g, me], ret_self_sem.at[g]).start()

    loop(0, NG, attend)

    def unpack(g):
        back_all(g).wait_recv()
        pltpu.make_async_copy(ret_out.at[g, me], ret_in.at[g, me], ret_self_sem.at[g]).wait()
        head = head_of((TOK, ROWS), 1)
        chosen = back_place[g]
        zero = jnp.zeros_like(chosen)
        left = jnp.concatenate([jnp.where(head == h, chosen, zero) for h in range(GH)], axis=0)
        home = dot(left, ret_in[g].reshape(ROWS, BACK)).astype(BF16)
        for t, ref in enumerate((dq_ref, dk_ref, dv_ref)):
            for h in range(GH):
                cols = pl.ds(pl.multiple_of((g * GH + h) * HD, HD), HD)
                ref[0, :, cols] = home[h * TOK : (h + 1) * TOK, t * HD : (t + 1) * HD]

    unpack(0)

    @pl.when(core == 1)
    def _():
        gain_plane(1)

    unpack(1)
    unpack(2)
    unpack(3)

    @pl.when(core == 0)
    def _():
        for n in range(2):
            plane_all(n, N_SEQ // 2).wait_recv()
            chip_copy(n).wait_send()

    @pl.when(core == 1)
    def _():
        for n in range(2):
            plane_all(n, N_SEQ // 2 - 1).wait_recv()
            along_all(n).wait_send()
            plane_all(n, N_SEQ // 2 - 1).wait_send()
            plane_all(n, N_SEQ // 2).wait_send()

    for n in range(2):
        gg_ref[n * 8 : (n + 1) * 8, :] = jnp.sum(p_in[n], axis=0)

    def finish(g):
        forward_all(g).wait_send()
        back_all(g).wait_send()

    loop(0, NG, finish)
    label_all().wait_send()


def hand_over(a, b, c, d, oa, ob, oc, od, sem):
    copies = [
        pltpu.make_async_copy(src, dst, sem.at[i])
        for i, (src, dst) in enumerate(zip((a, b, c, d), (oa, ob, oc, od)))
    ]
    for copy in copies:
        copy.start()
    for copy in copies:
        copy.wait()


def on_device(queries, keys, values, d_out, cluster_ids, gain):
    anywhere = pl.BlockSpec(memory_space=pl.ANY)
    in_vmem = pl.BlockSpec(memory_space=pltpu.VMEM)
    rows = jax.ShapeDtypeStruct(queries.shape, BF16)
    dma = pltpu.SemaphoreType.DMA
    query_grad, key_grad, value_grad, gain_grad = pl.pallas_call(
        kernel,
        out_shape=(rows, rows, rows, jax.ShapeDtypeStruct((H, HD), F32)),
        in_specs=[anywhere] * 4 + [pl.BlockSpec(memory_space=pltpu.HBM), in_vmem],
        out_specs=(in_vmem,) * 4,
        scratch_shapes=[
            pltpu.VMEM((NG, 4, TOK, GH * HD), BF16),
            pltpu.VMEM((H, TOK), jnp.int32),
            pltpu.VMEM((NG, ROWS, TOK), BF16),
            pltpu.VMEM((NG, TOK, ROWS), BF16),
            pltpu.VMEM((NG, N_SEQ, MSG, WIDE), BF16),
            pltpu.VMEM((NG, N_SEQ, MSG, WIDE), BF16),
            pltpu.VMEM((NG, N_SEQ, MSG, BACK), BF16),
            pltpu.VMEM((NG, N_SEQ, MSG, BACK), BF16),
            pltpu.VMEM((N_SEQ, HD), F32),
            pltpu.VMEM((N_SEQ, HD), F32),
            pltpu.VMEM((ROWS, ROWS), BF16),
            pltpu.VMEM((ROWS, ROWS), BF16),
            pltpu.VMEM((2, 8, HD), F32),
            pltpu.VMEM((2, 8, HD), F32),
            pltpu.VMEM((2, 8, HD), F32),
            pltpu.VMEM((2, N_DP, 8, HD), F32),
            pltpu.VMEM((2, 8, HD), F32),
            pltpu.VMEM((2, N_SEQ // 2, 8, HD), F32),
            dma((NG,)), dma, dma((NG,)), dma((NG,)), dma, pltpu.SemaphoreType.REGULAR,
            dma((NG,)), dma((NG,)), dma((NG,)), dma((NG,)), dma, dma,
            dma((2,)), dma((2,)), dma((2,)), dma((2,)), dma((2,)), dma((2,)),
        ],
        compiler_params=pltpu.CompilerParams(
            collective_id=0, has_side_effects=True, vmem_limit_bytes=52 * 2**20
        ),
    )(queries, keys, values, d_out, pltpu.with_memory_space_constraint(cluster_ids.swapaxes(1, 2), pltpu.HBM), pltpu.with_memory_space_constraint(gain.reshape(H, HD), pltpu.HBM))
    query_grad, key_grad, value_grad, gain_grad = pl.pallas_call(
        hand_over,
        out_shape=(rows, rows, rows, jax.ShapeDtypeStruct((H, HD), F32)),
        in_specs=[in_vmem] * 4,
        out_specs=(anywhere,) * 4,
        scratch_shapes=[dma((4,))],
        compiler_params=pltpu.CompilerParams(vmem_limit_bytes=4 * 2**20),
    )(query_grad, key_grad, value_grad, gain_grad)
    return query_grad, key_grad, value_grad, gain_grad.reshape(H * HD)


def solution(mesh):
    rows = P("dp", "seq", None)
    return jax.shard_map(
        on_device, mesh=mesh, in_specs=(rows,) * 5 + (P(),),
        out_specs=(rows, rows, rows, P()), check_vma=False,
    )
```
